32 devices in a mesh: section: 2 (over core), expert: 4 (over z), mp: 4 (over y, x).
Axes of the slice: x: 2, y: 2, z: 4, core: 2. Of those that a mesh axis runs over, the one named last changes fastest.
Arguments:
- layer_inputs: bfloat16 [2, 1024, 2048], P('section', ('expert', 'mp')), may hold values from -6 to 6
- norm_gain: float32 [2, 2048], P('section'), may hold values from 0.1 to 1.9
- w_gate: bfloat16 [2, 64, 768, 2048], P('section', 'expert', 'mp'), may hold values from -0.125 to 0.125
- w_up: bfloat16 [2, 64, 768, 2048], P('section', 'expert', 'mp'), may hold values from -0.125 to 0.125
- w_down: bfloat16 [2, 64, 768, 2048], P('section', 'expert', 'mp'), may hold values from -0.21875 to 0.21875
- routes: int32 [2, 1024, 8], P('section', ('expert', 'mp')), may hold values from 0 to 63, all different within a row; in each aligned block of 32 rows (0 to 31, 32 to 63, ..., all dimensions but the last counted through in order) at most 5 rows name the same one
- probs: float32 [2, 1024, 8], P('section', ('expert', 'mp')), may hold values from 0.05 to 0.3
- cotangent: bfloat16 [1024, 2048], P(('expert', 'mp')), may hold values from -6 to 6
- sampled: int32 [1], replicated, may hold values from 0 to 1
Outputs:
- input_grads: bfloat16 [2, 1024, 2048], P('section', ('expert', 'mp'))
- gate_grads: float32 [2, 64, 768, 2048], P('section', 'expert', 'mp')
- up_grads: float32 [2, 64, 768, 2048], P('section', 'expert', 'mp')
The draws below stay inside these ranges and needn't reach their ends.
Inputs may be any that keep to these rules, and one draw needn't show every extreme that they name: `routes`: each row names 8 different experts and every expert is named somewhere. In each aligned block of 32 rows of a layer, no expert is named by more than 5 rows, and in some blocks one expert is named by exactly 5.
All inputs are finite; a program needn't handle non-finite values.
Results may differ from the reference program's by a relative error of at most 0.012.
Values may be sent and summed in bfloat16 or wider, within the bound.
A program may use at most 384 MiB of HBM per device.

```python
import math
import jax
import jax.numpy as jnp
import numpy as np
from jax import lax

D = 2048
FF = 768
TOP = 8
EXPERTS = 64
TOK_DEV = 64
CAPH = 5
TOKENS = 1024
N_EXPERT = 4
N_MP = 4


def steps_of(key, extent, shards, smallest, largest):
    level, own = 1.0, jax.random.fold_in(key, 6)
    for position, blocks in shards:
        steps = jnp.exp(jax.random.uniform(jax.random.fold_in(own, position), (blocks,), jnp.float32, smallest / len(shards), largest / len(shards)))
        level = level * jnp.repeat(steps, extent[position] // blocks).reshape([-1 if axis == position else 1 for axis in range(len(extent))])
    return level


def shared_out(own_key, own, number, rows, count, top, most, slope):
    sequence = jax.random.permutation(own_key, count)
    crowded, ordinary = load_shares(count, rows * top, most, slope, True), load_shares(count, rows * top, most, slope, False)
    places = jnp.arange(count)

    def named(tallies, rotation):
        used = int((tallies > 0).sum())
        fixed = max(1, used // 4)
        moved = fixed + (places - fixed + rotation * (used - fixed)) % max(1, count - fixed)
        return jnp.zeros((count,), jnp.int32).at[sequence[jnp.where(places < fixed, places, moved)]].set(jnp.asarray(tallies, jnp.int32))

    tallies = jnp.where(number % 4 == 0, named(crowded, number // 4), named(ordinary, number - number // 4 - 1))
    mixed = jax.random.permutation(jax.random.fold_in(own, 3), count)
    donor, receiver = mixed[0:count // 2 * 2:2], mixed[1:count // 2 * 2:2]
    room = jnp.minimum(tallies[donor] - 1, most - tallies[receiver]) // 2
    room = jnp.where((donor == sequence[0]) | (receiver == sequence[0]) | (tallies[receiver] == 0), 0, jnp.maximum(room, 0))
    moved = jax.random.randint(jax.random.fold_in(own, 4), (count // 2,), 0, 1 << 20) % (room + 1)
    tallies = tallies.at[donor].add(-moved).at[receiver].add(moved)
    members = jnp.searchsorted(jnp.cumsum(tallies), jnp.arange(rows * top), side="right").astype(jnp.int32)
    table = members.reshape(top, rows).T
    table = table[jax.random.permutation(jax.random.fold_in(own, 1), rows)]
    rotation = jax.random.randint(jax.random.fold_in(own, 2), (rows, 1), 0, top)
    return jnp.take_along_axis(table, (jnp.arange(top)[None, :] + rotation) % top, axis=1)


def load_shares(amount, total, most, skew, full):
    portions = [(1 << 20) // math.isqrt(grade ** skew) + 1 for grade in range(1, amount + 1)]
    largest = most if full else min(most, max(-(-total // amount), total * portions[0] // sum(portions)))
    least = 1 if total - largest >= amount - 1 else 0
    counts, surplus = [largest] + [least] * (amount - 1), total - largest - least * (amount - 1)
    while surplus > 0:
        free = [i for i in range(1, amount) if counts[i] < largest] or [i for i in range(1, amount) if counts[i] < most]
        mass, remaining = sum([portions[i] for i in free]), surplus
        for i in free:
            extra = min(most - counts[i], max(1, remaining * portions[i] // mass), surplus)
            counts[i] = counts[i] + extra
            surplus = surplus - extra
    return np.array(counts)


def normal_values(own_key, extent, width, reach, shards=(), kind=jnp.bfloat16):
    drawn = width * jax.random.normal(own_key, extent, jnp.float32)
    if shards:
        drawn = drawn * steps_of(own_key, extent, shards, -0.22, 0.18)
    return jnp.clip(drawn, -reach, reach).astype(kind)


def setup_inputs(seed: int = 0) -> dict:
    splits = jax.random.split(jax.random.key(seed), 10)
    layer_inputs = normal_values(splits[0], (2, TOKENS, D), 1.0, 6.0, ((0, 2), (1, 16)))
    norm_gain = jnp.clip(1.0 + 0.18 * jax.random.normal(splits[1], (2, D), jnp.float32), 0.1, 1.9)
    w_gate = normal_values(splits[2], (2, EXPERTS, FF, D), D ** -0.5, 0.125, ((0, 2), (1, 4), (2, 4)))
    w_up = normal_values(splits[3], (2, EXPERTS, FF, D), D ** -0.5, 0.125, ((0, 2), (1, 4), (2, 4)))
    w_down = normal_values(splits[4], (2, EXPERTS, FF, D), FF ** -0.5, 0.21875, ((0, 2), (1, 4), (2, 4)))
    routes_keys = jax.random.split(jax.random.fold_in(splits[5], 1), 2 * TOKENS // (TOK_DEV // 2))
    routes_turns = jax.random.permutation(jax.random.fold_in(splits[5], 3), 2 * TOKENS // (TOK_DEV // 2))
    routes = jax.vmap(lambda own, number: shared_out(jax.random.fold_in(splits[5], 2), own, number, TOK_DEV // 2, EXPERTS, TOP, CAPH, 2))(routes_keys, routes_turns).reshape((2, TOKENS, TOP))
    probs = jnp.clip(0.05 + 0.25 * jax.random.uniform(splits[6], (2, TOKENS, TOP), jnp.float32) ** steps_of(splits[6], (2, TOKENS, TOP), ((0, 2), (1, 16)), -0.2, 0.2), 0.05, 0.3)
    cotangent = normal_values(splits[7], (TOKENS, D), 1.0, 6.0, ((0, 16),))
    sampled = jax.random.randint(splits[8], (1,), 0, 2).astype(jnp.int32)
    return dict(layer_inputs=layer_inputs, norm_gain=norm_gain, w_gate=w_gate, w_up=w_up, w_down=w_down, routes=routes, probs=probs, cotangent=cotangent, sampled=sampled)


epsilon = 1e-06

def normalize(inputs, gain_vector):
    values = inputs.astype(jnp.float32)
    factor = lax.rsqrt(lax.optimization_barrier(jnp.mean(values * values, axis=1, keepdims=True)) + epsilon)
    normed = values * factor
    return (normed, factor, (normed * gain_vector[None, :]).astype(jnp.bfloat16))

def expert_terms(operands, training):
    hidden_rows, weighted_rows, gate_w, up_w, down_w = operands
    gate_act = jnp.dot(hidden_rows, gate_w.T, preferred_element_type=jnp.float32)
    lifted = jnp.dot(hidden_rows, up_w.T, preferred_element_type=jnp.float32)
    back = jnp.dot(weighted_rows, down_w.T, preferred_element_type=jnp.float32)
    logistic = jax.nn.sigmoid(gate_act)
    d_gate = (back * lifted * logistic * (1.0 + gate_act * (1.0 - logistic))).astype(jnp.bfloat16)
    d_up = (back * gate_act * logistic).astype(jnp.bfloat16)
    slot_grad = (jnp.dot(d_gate, gate_w, preferred_element_type=jnp.float32) + jnp.dot(d_up, up_w, preferred_element_type=jnp.float32)).astype(jnp.bfloat16)

    def compute_grads():
        return (jnp.dot(d_gate.T, hidden_rows, preferred_element_type=jnp.float32), jnp.dot(d_up.T, hidden_rows, preferred_element_type=jnp.float32))

    def zero_grads():
        return (jnp.zeros((FF, D), jnp.float32), jnp.zeros((FF, D), jnp.float32))
    grad_gate, grad_up = lax.cond(training, compute_grads, zero_grads)
    return (slot_grad, grad_gate, grad_up)

def group_backward(inputs, gain_vector, gate_w, up_w, down_w, group_routes, group_probs, upstream, training):
    normed, factor, hidden = normalize(inputs, gain_vector)
    token_count = inputs.shape[0]
    limit = token_count // (TOK_DEV // 2) * CAPH
    flat_routes = group_routes.reshape(-1).astype(jnp.int32)
    onehot = (flat_routes[:, None] == jnp.arange(EXPERTS, dtype=jnp.int32)[None, :]).astype(jnp.int32)
    earlier = jnp.cumsum(onehot, axis=0) - onehot
    places = lax.optimization_barrier(jnp.sum(earlier * onehot, axis=1)).astype(jnp.int32)
    targets = (flat_routes * limit + places).astype(jnp.int32)
    hidden_slots = jnp.repeat(hidden, TOP, axis=0)
    weighted = (group_probs[:, :, None] * upstream[:, None, :].astype(jnp.float32)).astype(jnp.bfloat16)
    weighted = weighted.reshape(token_count * TOP, D)
    hidden_buffer = jnp.zeros((EXPERTS * limit, D), jnp.bfloat16).at[targets].set(hidden_slots).reshape(EXPERTS, limit, D)
    weighted_buffer = jnp.zeros((EXPERTS * limit, D), jnp.bfloat16).at[targets].set(weighted).reshape(EXPERTS, limit, D)
    slot_grads, grad_gate, grad_up = lax.map(lambda operands: expert_terms(operands, training), (hidden_buffer, weighted_buffer, gate_w, up_w, down_w))
    slot_values = slot_grads.reshape(EXPERTS * limit, D)[targets]
    token_grad = lax.optimization_barrier(jnp.sum(slot_values.reshape(token_count, TOP, D).astype(jnp.float32), axis=1))
    scaled = token_grad * gain_vector[None, :]
    inner = lax.optimization_barrier(jnp.mean(scaled * normed, axis=1, keepdims=True))
    input_grad = (upstream.astype(jnp.float32) + factor * (scaled - normed * inner)).astype(jnp.bfloat16)
    return (input_grad, grad_gate, grad_up)

def layer_backward(inputs, gain_vector, gate_w, up_w, down_w, layer_routes, layer_probs, upstream, training):

    def select(array, group):
        shaped = array.reshape((N_EXPERT, N_MP, TOK_DEV) + array.shape[1:])
        return shaped[:, group].reshape((N_EXPERT * TOK_DEV,) + array.shape[1:])
    grads_list = []
    gate_total = jnp.zeros((EXPERTS, FF, D), jnp.float32)
    up_total = jnp.zeros((EXPERTS, FF, D), jnp.float32)
    for group in range(N_MP):
        group_grad, group_gate, group_up = group_backward(select(inputs, group), gain_vector, gate_w, up_w, down_w, select(layer_routes, group), select(layer_probs, group), select(upstream, group), training)
        grads_list.append(group_grad.reshape(N_EXPERT, TOK_DEV, D))
        gate_total = gate_total + lax.optimization_barrier(group_gate.astype(jnp.bfloat16)).astype(jnp.float32)
        up_total = up_total + lax.optimization_barrier(group_up.astype(jnp.bfloat16)).astype(jnp.float32)
    input_grad = jnp.stack(grads_list, axis=1).reshape(N_EXPERT * N_MP * TOK_DEV, D)
    return (input_grad, gate_total, up_total)

def reference(layer_inputs, norm_gain, w_gate, w_up, w_down, routes, probs, cotangent, sampled):
    upper_grad, upper_gate, upper_up = layer_backward(layer_inputs[1], norm_gain[1], w_gate[1], w_up[1], w_down[1], routes[1], probs[1], cotangent, sampled[0] == 1)
    lower_grad, lower_gate, lower_up = layer_backward(layer_inputs[0], norm_gain[0], w_gate[0], w_up[0], w_down[0], routes[0], probs[0], upper_grad, sampled[0] == 0)
    return (jnp.stack([lower_grad, upper_grad]), jnp.stack([lower_gate, upper_gate]), jnp.stack([lower_up, upper_up]))
```

```python
import jax
import jax.numpy as jnp
from jax import lax
from jax.sharding import PartitionSpec as P

CAPH = 5


epsilon = 1e-06

OWNERS = ("expert", "mp")


def normalize(inputs, gain_vector):
    values = inputs.astype(jnp.float32)
    factor = lax.rsqrt(jnp.mean(values * values, axis=1, keepdims=True) + epsilon)
    normed = values * factor
    return (normed, factor, (normed * gain_vector[None, :]).astype(jnp.bfloat16))


def half_of(x, section_index):
    width = x.shape[-1] // 2
    return lax.dynamic_slice_in_dim(x, section_index * width, width, x.ndim - 1)


def swapped(x):
    return lax.ppermute(x, "section", [(0, 1), (1, 0)])


def joined(mine, other, section_index):
    first = jnp.where(section_index == 0, mine, other)
    second = jnp.where(section_index == 0, other, mine)
    return jnp.concatenate([first, second], axis=-1)


def gather_halves(rows, target, section_index):
    mine = lax.all_gather(half_of(rows, section_index), OWNERS, axis=0, tiled=True)
    other = lax.ppermute(mine, "section", [(1 - target, target)])
    return joined(mine, other, section_index)


def reduce_halves(partial, source, section_index):
    width = partial.shape[-1] // 2
    away, kept = (partial[:, :width], partial[:, width:])
    if source == 0:
        away, kept = (kept, away)
    other = lax.ppermute(away, "section", [(source, 1 - source)])
    mine = jnp.where(section_index == source, kept, other)
    total = lax.psum_scatter(mine, OWNERS, scatter_dimension=0, tiled=True)
    return joined(total, swapped(total), section_index).astype(jnp.float32)


def running_count(present, block_rows):
    counted = present.astype(jnp.bfloat16).reshape(present.shape[0], -1, block_rows)
    inside = jnp.triu(jnp.ones((block_rows, block_rows), jnp.bfloat16))
    within = jnp.einsum("ebi,ij->ebj", counted, inside, preferred_element_type=jnp.float32)
    totals = within[:, :, -1].astype(jnp.bfloat16)
    before = jnp.triu(jnp.ones((totals.shape[1], totals.shape[1]), jnp.bfloat16), 1)
    offset = jnp.einsum("eb,bj->ej", totals, before, preferred_element_type=jnp.float32)
    return (within + offset[:, :, None]).reshape(present.shape).astype(jnp.int32)


def finish(token_grad, gain_vector, normed, factor, upstream):
    scaled = token_grad * gain_vector[None, :]
    inner = jnp.mean(scaled * normed, axis=1, keepdims=True)
    return (upstream.astype(jnp.float32) + factor * (scaled - normed * inner)).astype(jnp.bfloat16)


def per_device(layer_inputs, norm_gain, w_gate, w_up, w_down, routes, probs, cotangent, sampled):
    section_index = lax.axis_index("section")
    gate_w, up_w, down_w = (w_gate[0], w_up[0], w_down[0])
    tok_rows, feature_width = cotangent.shape
    local_experts, units, _ = gate_w.shape
    tokens = tok_rows * lax.axis_size("expert") * lax.axis_size("mp")
    capacity = tokens // (tok_rows // 2) * CAPH
    top_count = routes.shape[2]
    training = sampled[0] == section_index

    gain_vector = norm_gain[0]
    normed, factor, hidden = normalize(layer_inputs[0], gain_vector)
    upper_inputs = swapped(layer_inputs[0])
    upper_gain = swapped(norm_gain[0])

    meta = jnp.concatenate([routes[0].astype(jnp.float32), probs[0]], axis=1)
    meta = lax.all_gather(meta, OWNERS, axis=0, tiled=True)
    all_routes = meta[:, :top_count].astype(jnp.int32)
    all_probs = meta[:, top_count:]
    hidden_all = lax.all_gather(hidden, OWNERS, axis=0, tiled=True)
    cot_all = gather_halves(cotangent, 1, section_index)

    own = lax.axis_index("expert") * local_experts + jnp.arange(local_experts, dtype=jnp.int32)
    match = all_routes[None, :, :] == own[:, None, None]
    present = jnp.any(match, axis=2)
    weight = jnp.sum(jnp.where(match, all_probs[None], 0.0), axis=2)
    place = running_count(present, tok_rows) - 1
    place = jnp.where(present, place, -1)
    spots = jnp.arange(capacity, dtype=jnp.int32)
    picked = place[:, None, :] == spots[None, :, None]
    dispatch = picked.astype(jnp.bfloat16)
    slot_prob = jnp.sum(jnp.where(picked, weight[:, None, :], 0.0), axis=2)

    rows = jnp.einsum(
        "ect,td->ecd", dispatch, hidden_all, preferred_element_type=jnp.float32
    ).astype(jnp.bfloat16)
    gate_act = jnp.einsum("ecd,efd->ecf", rows, gate_w, preferred_element_type=jnp.float32)
    lifted = jnp.einsum("ecd,efd->ecf", rows, up_w, preferred_element_type=jnp.float32)

    def layer_pass(upstream_all):
        up_rows = jnp.einsum(
            "ect,td->ecd", dispatch, upstream_all, preferred_element_type=jnp.float32
        )
        weighted = (slot_prob[:, :, None] * up_rows).astype(jnp.bfloat16)
        back = jnp.einsum("ecd,efd->ecf", weighted, down_w, preferred_element_type=jnp.float32)
        logistic = jax.nn.sigmoid(gate_act)
        d_gate = (back * lifted * logistic * (1.0 + gate_act * (1.0 - logistic))).astype(
            jnp.bfloat16
        )
        d_up = (back * gate_act * logistic).astype(jnp.bfloat16)
        slot_grad = jnp.einsum("ecf,efd->ecd", d_gate, gate_w, preferred_element_type=jnp.float32)
        slot_grad = slot_grad + jnp.einsum(
            "ecf,efd->ecd", d_up, up_w, preferred_element_type=jnp.float32
        )
        partial = jnp.einsum(
            "ect,ecd->td",
            dispatch,
            slot_grad.astype(jnp.bfloat16),
            preferred_element_type=jnp.float32,
        ).astype(jnp.bfloat16)
        return (partial, d_gate, d_up)

    def idle(upstream_all):
        empty = jnp.zeros((local_experts, capacity, units), jnp.bfloat16)
        return (jnp.zeros((tokens, feature_width), jnp.bfloat16), empty, empty)

    partial, gate_upper, up_upper = lax.cond(section_index == 1, layer_pass, idle, cot_all)
    token_grad = reduce_halves(partial, 1, section_index)
    top_inputs = jnp.where(section_index == 1, layer_inputs[0], upper_inputs)
    top_gain = jnp.where(section_index == 1, gain_vector, upper_gain)
    top_normed, top_factor, _ = normalize(top_inputs, top_gain)
    upper_grad = finish(token_grad, top_gain, top_normed, top_factor, cotangent)

    upper_all = gather_halves(upper_grad, 0, section_index)
    partial, gate_lower, up_lower = lax.cond(section_index == 0, layer_pass, idle, upper_all)
    token_grad = reduce_halves(partial, 0, section_index)
    lower_grad = finish(token_grad, gain_vector, normed, factor, upper_grad)
    result = jnp.where(section_index == 1, upper_grad, lower_grad)

    def weigh_rows(operands):
        gate_in, up_in, rows_in = operands
        return (
            jnp.einsum("ecf,ecd->efd", gate_in, rows_in, preferred_element_type=jnp.float32),
            jnp.einsum("ecf,ecd->efd", up_in, rows_in, preferred_element_type=jnp.float32),
        )

    def zero_rows(operands):
        empty = jnp.zeros((local_experts, units, feature_width), jnp.float32)
        return (empty, empty)

    d_gate = jnp.where(section_index == 1, gate_upper, gate_lower)
    d_up = jnp.where(section_index == 1, up_upper, up_lower)
    gate_share, up_share = lax.cond(training, weigh_rows, zero_rows, (d_gate, d_up, rows))
    return (result[None], gate_share[None], up_share[None])


def solution(mesh):
    placed = (
        P("section", OWNERS, None),
        P("section", None),
        P("section", "expert", "mp", None),
        P("section", "expert", "mp", None),
        P("section", "expert", "mp", None),
        P("section", OWNERS, None),
        P("section", OWNERS, None),
        P(OWNERS, None),
        P(),
    )
    return jax.shard_map(
        per_device,
        mesh=mesh,
        in_specs=placed,
        out_specs=(
            P("section", OWNERS, None),
            P("section", "expert", "mp", None),
            P("section", "expert", "mp", None),
        ),
        check_vma=False,
    )
```

```python
import jax
import jax.numpy as jnp
from jax import lax
from jax.sharding import PartitionSpec as P

CAPH = 5


epsilon = 1e-06

OWNERS = ("expert", "mp")


def pack_meta(own_routes, own_probs):
    high = lax.reduce_precision(own_probs, 8, 7)
    middle = lax.reduce_precision(own_probs - high, 8, 7)
    low = own_probs - high - middle
    digits = [(own_routes // 128).astype(jnp.float32), (own_routes % 128).astype(jnp.float32)]
    packed = jnp.concatenate(digits + [high, middle, low], axis=1).astype(jnp.bfloat16)
    return jnp.pad(packed, ((0, 0), (0, -packed.shape[1] % 128)))


def unpack_meta(packed, count):
    values = packed[:, : 5 * count].astype(jnp.float32)
    parts = [values[:, i * count : (i + 1) * count] for i in range(5)]
    return ((parts[0] * 128.0 + parts[1]).astype(jnp.int32), parts[2] + parts[3] + parts[4])


def normalize(inputs, gain_vector):
    values = inputs.astype(jnp.float32)
    factor = lax.rsqrt(jnp.mean(values * values, axis=1, keepdims=True) + epsilon)
    normed = values * factor
    return (normed, factor, (normed * gain_vector[None, :]).astype(jnp.bfloat16))


def half_of(x, section_index):
    width = x.shape[-1] // 2
    return lax.dynamic_slice_in_dim(x, section_index * width, width, x.ndim - 1)


def swapped(x):
    return lax.ppermute(x, "section", [(0, 1), (1, 0)])


def joined(mine, other, section_index):
    first = jnp.where(section_index == 0, mine, other)
    second = jnp.where(section_index == 0, other, mine)
    return jnp.concatenate([first, second], axis=-1)


def gather_halves(rows, target, section_index):
    mine = lax.all_gather(half_of(rows, section_index), OWNERS, axis=0, tiled=True)
    other = lax.ppermute(mine, "section", [(1 - target, target)])
    return joined(mine, other, section_index)


def reduce_halves(partial, source, section_index):
    width = partial.shape[-1] // 2
    away, kept = (partial[:, :width], partial[:, width:])
    if source == 0:
        away, kept = (kept, away)
    other = lax.ppermute(away, "section", [(source, 1 - source)])
    mine = jnp.where(section_index == source, kept, other)
    return lax.psum_scatter(mine, OWNERS, scatter_dimension=0, tiled=True)


def whole_rows(total, section_index):
    return joined(total, swapped(total), section_index).astype(jnp.float32)


def running_count(present, block_rows):
    counted = present.astype(jnp.bfloat16).reshape(present.shape[0], -1, block_rows)
    inside = jnp.triu(jnp.ones((block_rows, block_rows), jnp.bfloat16))
    within = jnp.einsum("ebi,ij->ebj", counted, inside, preferred_element_type=jnp.float32)
    totals = within[:, :, -1].astype(jnp.bfloat16)
    before = jnp.triu(jnp.ones((totals.shape[1], totals.shape[1]), jnp.bfloat16), 1)
    offset = jnp.einsum("eb,bj->ej", totals, before, preferred_element_type=jnp.float32)
    return (within + offset[:, :, None]).reshape(present.shape).astype(jnp.int32)


def finish(token_grad, gain_vector, normed, factor, upstream):
    scaled = token_grad * gain_vector[None, :]
    inner = jnp.mean(scaled * normed, axis=1, keepdims=True)
    return (upstream.astype(jnp.float32) + factor * (scaled - normed * inner)).astype(jnp.bfloat16)


def per_device(layer_inputs, norm_gain, w_gate, w_up, w_down, routes, probs, cotangent, sampled):
    section_index = lax.axis_index("section")
    gate_w, up_w, down_w = (w_gate[0], w_up[0], w_down[0])
    tok_rows, feature_width = cotangent.shape
    local_experts, units, _ = gate_w.shape
    tokens = tok_rows * lax.axis_size("expert") * lax.axis_size("mp")
    capacity = tokens // (tok_rows // 2) * CAPH
    top_count = routes.shape[2]
    training = sampled[0] == section_index

    gain_vector = norm_gain[0]
    normed, factor, hidden = normalize(layer_inputs[0], gain_vector)
    upper_inputs = swapped(layer_inputs[0])
    upper_gain = swapped(norm_gain[0])

    sent = jnp.concatenate([hidden, pack_meta(routes[0], probs[0])], axis=1)
    sent_all = lax.all_gather(sent, OWNERS, axis=0, tiled=True)
    hidden_all = sent_all[:, :feature_width]
    all_routes, all_probs = unpack_meta(sent_all[:, feature_width:], top_count)
    cot_half = lax.all_gather(half_of(cotangent, section_index), OWNERS, axis=0, tiled=True)

    own = lax.axis_index("expert") * local_experts + jnp.arange(local_experts, dtype=jnp.int32)
    match = all_routes[None, :, :] == own[:, None, None]
    present = jnp.any(match, axis=2)
    weight = jnp.sum(jnp.where(match, all_probs[None], 0.0), axis=2)
    place = running_count(present, tok_rows) - 1
    place = jnp.where(present, place, -1)
    spots = jnp.arange(capacity, dtype=jnp.int32)
    picked = place[:, None, :] == spots[None, :, None]
    dispatch = picked.astype(jnp.bfloat16)
    slot_prob = jnp.sum(jnp.where(picked, weight[:, None, :], 0.0), axis=2)

    rows = jnp.einsum(
        "ect,td->ecd", dispatch, hidden_all, preferred_element_type=jnp.float32
    ).astype(jnp.bfloat16)
    gate_act = jnp.einsum("ecd,efd->ecf", rows, gate_w, preferred_element_type=jnp.float32)
    lifted = jnp.einsum("ecd,efd->ecf", rows, up_w, preferred_element_type=jnp.float32)

    cot_half, rows, gate_act, lifted = lax.optimization_barrier((cot_half, rows, gate_act, lifted))
    cot_other = lax.ppermute(cot_half, "section", [(0, 1)])
    cot_all = joined(cot_half, cot_other, section_index)

    def layer_pass(upstream_all):
        up_rows = jnp.einsum(
            "ect,td->ecd", dispatch, upstream_all, preferred_element_type=jnp.float32
        )
        weighted = (slot_prob[:, :, None] * up_rows).astype(jnp.bfloat16)
        back = jnp.einsum("ecd,efd->ecf", weighted, down_w, preferred_element_type=jnp.float32)
        logistic = jax.nn.sigmoid(gate_act)
        d_gate = (back * lifted * logistic * (1.0 + gate_act * (1.0 - logistic))).astype(
            jnp.bfloat16
        )
        d_up = (back * gate_act * logistic).astype(jnp.bfloat16)
        slot_grad = jnp.einsum("ecf,efd->ecd", d_gate, gate_w, preferred_element_type=jnp.float32)
        slot_grad = slot_grad + jnp.einsum(
            "ecf,efd->ecd", d_up, up_w, preferred_element_type=jnp.float32
        )
        partial = jnp.einsum(
            "ect,ecd->td",
            dispatch,
            slot_grad.astype(jnp.bfloat16),
            preferred_element_type=jnp.float32,
        ).astype(jnp.bfloat16)
        return (partial, d_gate, d_up)

    def idle(upstream_all):
        empty = jnp.zeros((local_experts, capacity, units), jnp.bfloat16)
        return (jnp.zeros((tokens, feature_width), jnp.bfloat16), empty, empty)

    partial, gate_upper, up_upper = lax.cond(section_index == 1, layer_pass, idle, cot_all)
    token_grad = whole_rows(reduce_halves(partial, 1, section_index), section_index)
    top_inputs = jnp.where(section_index == 1, layer_inputs[0], upper_inputs)
    top_gain = jnp.where(section_index == 1, gain_vector, upper_gain)
    top_normed, top_factor, _ = normalize(top_inputs, top_gain)
    upper_grad = finish(token_grad, top_gain, top_normed, top_factor, cotangent)

    upper_all = gather_halves(upper_grad, 0, section_index)
    partial, gate_lower, up_lower = lax.cond(section_index == 0, layer_pass, idle, upper_all)
    total = reduce_halves(partial, 0, section_index)

    def weigh_rows(operands):
        gate_in, up_in, rows_in = operands
        return (
            jnp.einsum("ecf,ecd->efd", gate_in, rows_in, preferred_element_type=jnp.float32),
            jnp.einsum("ecf,ecd->efd", up_in, rows_in, preferred_element_type=jnp.float32),
        )

    def zero_rows(operands):
        empty = jnp.zeros((local_experts, units, feature_width), jnp.float32)
        return (empty, empty)

    d_gate = jnp.where(section_index == 1, gate_upper, gate_lower)
    d_up = jnp.where(section_index == 1, up_upper, up_lower)
    gate_share, up_share = lax.cond(training, weigh_rows, zero_rows, (d_gate, d_up, rows))
    total, gate_share, up_share = lax.optimization_barrier((total, gate_share, up_share))
    token_grad = whole_rows(total, section_index)
    lower_grad = finish(token_grad, gain_vector, normed, factor, upper_grad)
    result = jnp.where(section_index == 1, upper_grad, lower_grad)
    return (result[None], gate_share[None], up_share[None])


def solution(mesh):
    placed = (
        P("section", OWNERS, None),
        P("section", None),
        P("section", "expert", "mp", None),
        P("section", "expert", "mp", None),
        P("section", "expert", "mp", None),
        P("section", OWNERS, None),
        P("section", OWNERS, None),
        P(OWNERS, None),
        P(),
    )
    return jax.shard_map(
        per_device,
        mesh=mesh,
        in_specs=placed,
        out_specs=(
            P("section", OWNERS, None),
            P("section", "expert", "mp", None),
            P("section", "expert", "mp", None),
        ),
        check_vma=False,
    )
```
